512 devices in a mesh: seq: 32 (over z, y_hi), fsdp: 16 (over x, y_lo, core).
Axes of the slice: x: 4, y: 8 (y_hi: 4, y_lo: 2; y = y_hi * 2 + y_lo), z: 8, core: 2. Of those that a mesh axis runs over, the one named last changes fastest.
Arguments:
- queries: bfloat16 [16, 6144, 768], P('fsdp', 'seq'), may hold values from -26 to 26
- keys: bfloat16 [16, 6144, 768], P('fsdp', 'seq'), may hold values from -26 to 26
- values: bfloat16 [16, 6144, 768], P('fsdp', 'seq'), may hold values from -6 to 6
- rec_lengths: int32 [16, 4], P('fsdp'), may hold values from 1 to 3072, 6144 in all within a row
- out_weight: bfloat16 [768, 1536], P('fsdp'), may hold values from -0.21875 to 0.21875
- cotangent: bfloat16 [16, 6144, 1536], P('fsdp', 'seq'), may hold values from -6 to 6
Outputs:
- attended: bfloat16 [16, 6144, 1536], P('fsdp', 'seq')
- grad_queries: bfloat16 [16, 6144, 768], P('fsdp', 'seq')
- grad_keys: bfloat16 [16, 6144, 768], P('fsdp', 'seq')
- grad_values: bfloat16 [16, 6144, 768], P('fsdp', 'seq')
- grad_weight: float32 [768, 1536], P('fsdp', 'seq')
The draws below stay inside these ranges and needn't reach their ends.
Inputs may be any that keep to these rules, and one draw needn't show every extreme that they name: `rec_lengths`: each row holds 4 lengths that sum to 6144; the recordings lie end to end in frame order.
All inputs are finite; a program needn't handle non-finite values.
Results may differ from the reference program's by a relative error of at most 0.029.
Values may be sent and summed in bfloat16 or wider, within the bound.
No kernel may reach another device: no remote copies, remote signals or barrier semaphores. Data moves between devices by JAX's collectives and lax.ppermute only.
A program may use at most 128 MiB of HBM per device.

```python
import math
import jax
import jax.numpy as jnp
import numpy as np
from jax import lax

D = 1536
HEADS = 8
HEAD_DIM = 96
ROWS = 192
HOPS = 2
RECS = 4
INNER = 768
FRAMES = 6144
BATCH = 16
N_SEQ = 32


def draw_queries(key, part):
    key = jax.random.fold_in(key, 21)
    drawn = jax.random.truncated_normal(key, -4.5, 4.5, (BATCH, FRAMES, INNER), jnp.float32)
    return drawn.astype(jnp.bfloat16)


def draw_keys(key, part):
    key = jax.random.fold_in(key, 22)
    drawn = jax.random.truncated_normal(key, -4.5, 4.5, (BATCH, FRAMES, INNER), jnp.float32)
    return drawn.astype(jnp.bfloat16)


def with_spikes(values, own_key, source, target, blocks, factor):
    owner, partner = [(jnp.arange(values.shape[dim]) // (values.shape[dim] // blocks)).reshape([-1 if axis == dim else 1 for axis in range(values.ndim)]) for dim in (source, target)]
    chosen = jax.random.permutation(own_key, blocks)[partner]
    strong = (owner == chosen) | (owner == (partner + blocks // 2) % blocks)
    return jnp.where(strong, factor * values, values)


def levels(key, dims, cuts, smallest, high):
    gain = 1.0
    for position, parts in cuts:
        draws = jax.random.uniform(jax.random.fold_in(jax.random.fold_in(key, 6), position), (parts,), jnp.float32, smallest / len(cuts), high / len(cuts))
        gain = gain * jnp.repeat(jnp.exp(draws), dims[position] // parts).reshape((-1,) + (1,) * (len(dims) - 1 - position))
    return gain


def profile(amount, total, limit, skew):
    weights = [(1 << 20) // math.isqrt(rank ** skew) + 1 for rank in range(2, amount + 1)]
    spare, holding = total - limit - (amount - 1), [1] * (amount - 1)
    while spare > 0:
        movable = [i for i in range(amount - 1) if holding[i] < limit]
        whole, left = sum([weights[i] for i in movable]), spare
        for i in movable:
            extra = min(limit - holding[i], max(1, left * weights[i] // whole), spare)
            holding[i] = holding[i] + extra
            spare = spare - extra
    return np.array([limit] + holding)


def ragged(stream_key, count, total, reach, skew):
    if count == 2:
        one = jax.random.randint(stream_key, (), max(1, total - reach), min(reach, total - 1) + 1)
        return jnp.stack([one, total - one])
    sizes = jnp.asarray(profile(count, total, reach, skew), jnp.int32)
    pairs = (count - 1) // 2
    giver, receiver = sizes[1:1 + 2 * pairs:2], sizes[2:2 + 2 * pairs:2]
    room = jnp.minimum(giver - 1, reach - receiver)
    shifted = jax.random.randint(jax.random.fold_in(stream_key, 1), (pairs,), 0, 1 << 20) % (room + 1)
    sizes = sizes.at[1:1 + 2 * pairs:2].set(giver - shifted).at[2:2 + 2 * pairs:2].set(receiver + shifted)
    return sizes[jax.random.permutation(jax.random.fold_in(stream_key, 2), count)]


def normal_values(own_key, extent, width, reach, shards=(), kind=jnp.bfloat16):
    drawn = width * jax.random.normal(own_key, extent, jnp.float32)
    if shards:
        drawn = drawn * levels(own_key, extent, shards, -0.22, 0.18)
    return jnp.clip(drawn, -reach, reach).astype(kind)


def gaussian_with(stream_key, extent, scale, limit, split, heavy, kind=jnp.bfloat16):
    entries = scale * jax.random.normal(stream_key, extent, jnp.float32)
    if split:
        entries = entries * levels(stream_key, extent, split, -0.22, 0.18)
    return jnp.clip(with_spikes(entries, jax.random.fold_in(stream_key, 3), *heavy), -limit, limit).astype(kind)


def setup_inputs(seed: int = 0) -> dict:
    arg_keys = jax.random.split(jax.random.key(seed), 7)
    return {
        "queries": draw_queries(jax.random.fold_in(arg_keys[6], 71), 0),
        "keys": draw_keys(jax.random.fold_in(arg_keys[6], 71), 0),
        "values": normal_values(arg_keys[2], (BATCH, FRAMES, INNER), 1.0, 6.0, ((0, 16), (1, 32))),
        "rec_lengths": jax.vmap(lambda own: ragged(own, RECS, FRAMES, FRAMES // 2, 2))(jax.random.split(arg_keys[3], BATCH)).reshape((BATCH, RECS)).astype(jnp.int32),
        "out_weight": normal_values(arg_keys[4], (INNER, D), INNER ** -0.5, 0.21875, ((0, 16),)),
        "cotangent": gaussian_with(arg_keys[5], (BATCH, FRAMES, D), 1.0, 6.0, ((0, 16), (1, 32)), (1, 2, 32, 2.75)),
    }


NEG_FILL = -1.0e30


def allowed(query_pos, key_pos, lengths, frames, window):
    ends = jnp.cumsum(lengths).astype(jnp.int32)
    query_rec = jnp.sum((query_pos[:, None] >= ends[None, :-1]).astype(jnp.int32), axis=1)
    key_rec = jnp.sum((key_pos[:, None] >= ends[None, :-1]).astype(jnp.int32), axis=1)
    inside = (key_pos >= 0) & (key_pos < frames)
    near = jnp.abs(query_pos[:, None] - key_pos[None, :]) <= window
    return inside[None, :] & near & (query_rec[:, None] == key_rec[None, :])


def split_heads(matrix):
    return matrix.reshape(matrix.shape[0], HEADS, HEAD_DIM).transpose(1, 0, 2)


def merge_heads(stacked):
    return stacked.transpose(1, 0, 2).reshape(stacked.shape[1], HEADS * HEAD_DIM)


def head_forward(query_head, key_head, value_head, allowed_mask):
    scale = HEAD_DIM ** -0.5
    scores = jnp.dot(query_head, key_head.T, preferred_element_type=jnp.float32) * scale
    scores = jnp.where(allowed_mask, scores, NEG_FILL)
    largest = jnp.max(scores, axis=1)
    expo = jnp.where(allowed_mask, jnp.exp(scores - largest[:, None]), 0.0)
    totals = jnp.sum(expo, axis=1)
    context = jnp.dot(expo.astype(jnp.bfloat16), value_head, preferred_element_type=jnp.float32) / totals[:, None]
    return context, largest + jnp.log(totals)


def attention_forward(query_rows, key_rows, value_rows, allowed_mask):
    def one_head(operands):
        return head_forward(operands[0], operands[1], operands[2], allowed_mask)

    context, log_total = lax.map(one_head, (split_heads(query_rows), split_heads(key_rows), split_heads(value_rows)))
    return merge_heads(context).astype(jnp.bfloat16), log_total


def head_backward(query_head, key_head, value_head, dcontext_head, log_total, delta, allowed_mask):
    scale = HEAD_DIM ** -0.5
    scores = jnp.dot(query_head, key_head.T, preferred_element_type=jnp.float32) * scale
    scores = jnp.where(allowed_mask, scores, NEG_FILL)
    probability = jnp.where(allowed_mask, jnp.exp(scores - log_total[:, None]), 0.0)
    product_grad = jnp.dot(dcontext_head, value_head.T, preferred_element_type=jnp.float32)
    score_grad = (probability * (product_grad - delta[:, None])).astype(jnp.bfloat16)
    grad_query = jnp.dot(score_grad, key_head, preferred_element_type=jnp.float32) * scale
    grad_key = jnp.dot(score_grad.T, query_head, preferred_element_type=jnp.float32) * scale
    grad_value = jnp.dot(probability.astype(jnp.bfloat16).T, dcontext_head, preferred_element_type=jnp.float32)
    return grad_query, grad_key, grad_value


def attention_backward(query_rows, key_rows, value_rows, dcontext, log_total, delta, allowed_mask):
    def one_head(operands):
        return head_backward(operands[0], operands[1], operands[2], operands[3], operands[4], operands[5], allowed_mask)

    grad_query, grad_key, grad_value = lax.map(one_head, (split_heads(query_rows), split_heads(key_rows), split_heads(value_rows), split_heads(dcontext), log_total, delta))
    return merge_heads(grad_query), jnp.concatenate([merge_heads(grad_key), merge_heads(grad_value)], axis=1)


def head_delta(dcontext, context):
    product = dcontext.astype(jnp.float32) * context.astype(jnp.float32)
    return jnp.sum(product.reshape(product.shape[0], HEADS, HEAD_DIM), axis=2).T


def one_stream(operands, out_weight):
    query_rows, key_rows, value_rows, lengths, cotangent = operands
    frames = ROWS * N_SEQ
    window = HOPS * ROWS
    span = (2 * HOPS + 1) * ROWS
    inner = HEADS * HEAD_DIM
    padding = ((window, window), (0, 0))
    key_pad = jnp.pad(key_rows, padding)
    value_pad = jnp.pad(value_rows, padding)

    def block(carry, block_index):
        key_value_acc, weight_acc = carry
        start = block_index * ROWS
        block_query = lax.dynamic_slice_in_dim(query_rows, start, ROWS, 0)
        block_key = lax.dynamic_slice_in_dim(key_pad, start, span, 0)
        block_value = lax.dynamic_slice_in_dim(value_pad, start, span, 0)
        block_cot = lax.dynamic_slice_in_dim(cotangent, start, ROWS, 0)
        query_pos = start + jnp.arange(ROWS, dtype=jnp.int32)
        key_pos = start - window + jnp.arange(span, dtype=jnp.int32)
        allowed_mask = allowed(query_pos, key_pos, lengths, frames, window)
        context, log_total = attention_forward(block_query, block_key, block_value, allowed_mask)
        attended = jnp.dot(context, out_weight, preferred_element_type=jnp.float32).astype(jnp.bfloat16)
        dcontext = lax.dot_general(block_cot, out_weight, (((1,), (1,)), ((), ())), preferred_element_type=jnp.float32).astype(jnp.bfloat16)
        delta = head_delta(dcontext, context)
        grad_query, grad_key_value = attention_backward(block_query, block_key, block_value, dcontext, log_total, delta, allowed_mask)
        current = lax.dynamic_slice_in_dim(key_value_acc, start, span, 0)
        key_value_acc = lax.dynamic_update_slice_in_dim(key_value_acc, current + grad_key_value, start, 0)
        term = lax.dot_general(context, block_cot, (((0,), (0,)), ((), ())), preferred_element_type=jnp.float32)
        rounded = lax.optimization_barrier(term.astype(jnp.bfloat16))
        weight_acc = weight_acc + rounded.astype(jnp.float32)
        return (key_value_acc, weight_acc), (attended, grad_query.astype(jnp.bfloat16))

    start_acc = (jnp.zeros((frames + 2 * window, 2 * inner), jnp.float32), jnp.zeros((inner, out_weight.shape[1]), jnp.float32))
    (key_value_acc, weight_acc), (attended, grad_query) = lax.scan(block, start_acc, jnp.arange(N_SEQ, dtype=jnp.int32))
    grad_key_value = key_value_acc[window:window + frames]
    attended = attended.reshape(frames, out_weight.shape[1])
    grad_query = grad_query.reshape(frames, inner)
    grad_key = grad_key_value[:, :inner].astype(jnp.bfloat16)
    grad_value = grad_key_value[:, inner:].astype(jnp.bfloat16)
    return attended, grad_query, grad_key, grad_value, weight_acc


def reference(queries, keys, values, rec_lengths, out_weight, cotangent):
    def stream(operands):
        return one_stream(operands, out_weight)

    attended, grad_queries, grad_keys, grad_values, weight_terms = lax.map(stream, (queries, keys, values, rec_lengths, cotangent))
    return attended, grad_queries, grad_keys, grad_values, jnp.sum(weight_terms, axis=0)
```

```python
import jax
import jax.numpy as jnp
from jax import lax
from jax.experimental import pallas as pl
from jax.experimental.pallas import tpu as pltpu
from jax.sharding import PartitionSpec as P

HEAD_DIM = 96
ROWS = 192
GROUP = 4
PAIR = 2 * HEAD_DIM
INNER = GROUP * PAIR
OWN = GROUP * ROWS
REACH = 2 * ROWS
SPAN = OWN + 2 * REACH
TILE = 256
WINDOW = TILE + 2 * REACH
STRIP = 48
WIDTH = 1536
SCALE = HEAD_DIM ** (-0.5)
LOG2E = 1.4426950408889634
NEG_FILL = -1e30
BF16 = jnp.bfloat16
F32 = jnp.float32


def struct(shape, dtype=BF16):
    return jax.ShapeDtypeStruct(shape, dtype)


def call(body, out_shape, args, flops=0, scratch=(), smem=1):
    vmem = pl.BlockSpec(memory_space=pltpu.VMEM)
    scalars = pl.BlockSpec(memory_space=pltpu.SMEM)
    moved = sum(a.size * a.dtype.itemsize for a in args)
    moved += sum(o.size * o.dtype.itemsize for o in jax.tree.leaves(out_shape))
    return pl.pallas_call(
        body,
        out_shape=out_shape,
        in_specs=[scalars] * smem + [vmem] * (len(args) - smem),
        out_specs=jax.tree.map(lambda _: vmem, out_shape),
        scratch_shapes=list(scratch),
        cost_estimate=pl.CostEstimate(flops=flops, bytes_accessed=moved, transcendentals=0),
        compiler_params=pltpu.CompilerParams(vmem_limit_bytes=40 * 1024 * 1024),
    )(*args)


def wrap(index):
    return lax.rem(index + 2 * GROUP, GROUP)


def rows_at(start, size):
    return pl.ds(pl.multiple_of(start, 16), size)


def dot(a, b):
    return jnp.dot(a, b, preferred_element_type=F32)


def dot_nt(a, b):
    return lax.dot_general(a, b, (((1,), (1,)), ((), ())), preferred_element_type=F32)


def pack_heads(pos, q, k, v, *outs):
    y = pos[0]
    for head_pair in range(GROUP):
        columns = slice(head_pair * PAIR, (head_pair + 1) * PAIR)
        hop = wrap(head_pair - y)
        for j in range(GROUP):

            @pl.when(hop == j)
            def _(j=j, columns=columns):
                outs[j][:, 0:PAIR] = k[0, :, columns]
                outs[j][:, PAIR : 2 * PAIR] = v[0, :, columns]
                outs[j][:, 2 * PAIR : 3 * PAIR] = q[0, :, columns]


def pack_edges(pos, *refs):
    parts, (low, high) = refs[:GROUP], refs[GROUP:]
    y = pos[0]
    for hop in range(GROUP):
        shard = wrap(y - hop)

        @pl.when(shard < 2)
        def _(hop=hop, shard=shard):
            low[rows_at(shard * ROWS, ROWS), :] = parts[hop][:, 0 : 2 * PAIR]

        @pl.when(shard >= 2)
        def _(hop=hop, shard=shard):
            high[rows_at((shard - 2) * ROWS, ROWS), :] = parts[hop][:, 0 : 2 * PAIR]


def tile_mask(lengths, first_query, frames):
    query = first_query + lax.broadcasted_iota(jnp.int32, (TILE, 1), 0)
    low = jnp.maximum(query - REACH, 0)
    high = jnp.minimum(query + REACH, frames - 1)
    end = 0
    for recording in range(3):
        end = end + lengths[0, recording]
        low = jnp.maximum(low, jnp.where(query >= end, end, 0))
        high = jnp.minimum(high, jnp.where(query < end, end - 1, frames - 1))
    key = first_query - REACH + lax.broadcasted_iota(jnp.int32, (1, WINDOW), 1)
    return (key >= low) & (key <= high)


def head_columns(head):
    lane = lax.broadcasted_iota(jnp.int32, (1, PAIR), 1)
    return (lane >= head * HEAD_DIM) & (lane < (head + 1) * HEAD_DIM)


def forward(frames, pos, lengths, *refs):
    parts = refs[:GROUP]
    before, after = refs[GROUP : GROUP + 2]
    outs = refs[GROUP + 2 : 2 * GROUP + 2]
    q_all, k_all, v_all, context, log_total = refs[2 * GROUP + 2 :]
    y, z = pos[0], pos[1]
    k_all[0:REACH, :] = before[:, 0:PAIR]
    v_all[0:REACH, :] = before[:, PAIR : 2 * PAIR]
    k_all[REACH + OWN : SPAN, :] = after[:, 0:PAIR]
    v_all[REACH + OWN : SPAN, :] = after[:, PAIR : 2 * PAIR]
    for hop in range(GROUP):
        start = wrap(y - hop) * ROWS
        k_all[rows_at(REACH + start, ROWS), :] = parts[hop][:, 0:PAIR]
        v_all[rows_at(REACH + start, ROWS), :] = parts[hop][:, PAIR : 2 * PAIR]
        q_all[rows_at(start, ROWS), :] = parts[hop][:, 2 * PAIR : 3 * PAIR]

    def step(tile, _):
        first = pl.multiple_of(tile * TILE, TILE)
        mask = tile_mask(lengths, z * OWN + first, frames)
        query = q_all[pl.ds(first, TILE), :]
        keys = k_all[pl.ds(first, WINDOW), :]
        values = v_all[pl.ds(first, WINDOW), :]
        lane = lax.broadcasted_iota(jnp.int32, (TILE, 128), 1)
        total = jnp.zeros((TILE, PAIR), F32)
        logs = jnp.zeros((TILE, 128), F32)
        for head in range(2):
            inside = head_columns(head)
            scores = dot_nt(jnp.where(inside, query, 0), keys)
            scores = jnp.where(mask, scores, NEG_FILL)
            largest = jnp.max(scores, axis=1, keepdims=True)
            expo = jnp.exp2((scores - largest) * (SCALE * LOG2E))
            sums = jnp.sum(expo, axis=1, keepdims=True)
            product = dot(expo.astype(BF16), values) / sums
            total = jnp.where(inside, product, total)
            logs = jnp.where(lane == head, largest + jnp.log(sums) * (1.0 / SCALE), logs)
        context[pl.ds(first, TILE), :] = total.astype(BF16)
        log_total[pl.ds(first, TILE), :] = logs
        return 0

    lax.fori_loop(0, OWN // TILE, step, 0)
    for hop in range(GROUP):
        outs[hop][...] = context[rows_at(wrap(y + hop) * ROWS, ROWS), :]


def backward(frames, pos, lengths, *refs):
    parts = refs[:GROUP]
    q_all, k_all, v_all, context, log_total = refs[GROUP : GROUP + 5]
    dq, own, low, high = refs[GROUP + 5 : GROUP + 9]
    dcontext, dk, dv = refs[GROUP + 9 :]
    y, z = pos[0], pos[1]
    for hop in range(GROUP):
        dcontext[rows_at(wrap(y - hop) * ROWS, ROWS), :] = parts[hop][...]
    dk[...] = jnp.zeros_like(dk)
    dv[...] = jnp.zeros_like(dv)

    def step(tile, _):
        first = pl.multiple_of(tile * TILE, TILE)
        mask = tile_mask(lengths, z * OWN + first, frames)
        query = q_all[pl.ds(first, TILE), :]
        keys = k_all[pl.ds(first, WINDOW), :]
        values = v_all[pl.ds(first, WINDOW), :]
        grads = dcontext[pl.ds(first, TILE), :]
        product = grads.astype(F32) * context[pl.ds(first, TILE), :].astype(F32)
        logs = log_total[pl.ds(first, TILE), :]
        query_t = query.T
        grads_t = grads.T
        total = jnp.zeros((TILE, PAIR), F32)
        for head in range(2):
            inside = head_columns(head)
            own_rows = slice(head * HEAD_DIM, (head + 1) * HEAD_DIM)
            delta = jnp.sum(jnp.where(inside, product, 0.0), axis=1, keepdims=True)
            scores = dot_nt(jnp.where(inside, query, 0), keys)
            scores = jnp.where(mask, scores, NEG_FILL)
            probability = jnp.exp2((scores - logs[:, head : head + 1]) * (SCALE * LOG2E))
            gap = dot_nt(jnp.where(inside, grads, 0), values) - delta
            score_grad = (probability * gap).astype(BF16)
            total = jnp.where(inside, dot(score_grad, keys), total)
            dk[own_rows, pl.ds(first, WINDOW)] += dot(query_t[own_rows, :], score_grad)
            dv[own_rows, pl.ds(first, WINDOW)] += dot(
                grads_t[own_rows, :], probability.astype(BF16)
            )
        dq[pl.ds(first, TILE), :] = (total * SCALE).astype(BF16)
        return 0

    lax.fori_loop(0, OWN // TILE, step, 0)
    low[:, 0:PAIR] = (dk[:, 0:REACH].T * SCALE).astype(BF16)
    low[:, PAIR : 2 * PAIR] = dv[:, 0:REACH].T.astype(BF16)
    high[:, 0:PAIR] = (dk[:, REACH + OWN : SPAN].T * SCALE).astype(BF16)
    high[:, PAIR : 2 * PAIR] = dv[:, REACH + OWN : SPAN].T.astype(BF16)
    own[:, 0:PAIR] = dk[:, REACH : REACH + OWN].T * SCALE
    own[:, PAIR : 2 * PAIR] = dv[:, REACH : REACH + OWN].T


def pack_grads(pos, dq, own, from_before, from_after, *refs):
    outs, total = refs[:GROUP], refs[GROUP]
    y = pos[0]
    total[0:REACH, :] = own[0:REACH, :] + from_before[...].astype(F32)
    total[REACH:OWN, :] = own[REACH:OWN, :] + from_after[...].astype(F32)
    for hop in range(GROUP):
        rows = rows_at(wrap(y + hop) * ROWS, ROWS)
        outs[hop][:, 0 : 2 * PAIR] = total[rows, :].astype(BF16)
        outs[hop][:, 2 * PAIR : 3 * PAIR] = dq[rows, :]


def unpack_grads(pos, *refs):
    parts, (dq, dk, dv) = refs[:GROUP], refs[GROUP:]
    y = pos[0]
    for hop in range(GROUP):
        shard = wrap(y - hop)
        for head_pair in range(GROUP):

            @pl.when(shard == head_pair)
            def _(hop=hop, head_pair=head_pair):
                columns = slice(head_pair * PAIR, (head_pair + 1) * PAIR)
                dk[0, :, columns] = parts[hop][:, 0:PAIR]
                dv[0, :, columns] = parts[hop][:, PAIR : 2 * PAIR]
                dq[0, :, columns] = parts[hop][:, 2 * PAIR : 3 * PAIR]


def context_grad(pos, cot, mine, other, *refs):
    outs, weight = refs[:GROUP], refs[GROUP]
    y, x, y_low, core = pos[0], pos[2], pos[3], pos[4]
    for j in range(4):
        for t in range(2):
            for flip, source in ((0, mine), (1, other)):
                strip = wrap(x - j) * 4 + (y_low + t) % 2 * 2 + (core + flip) % 2
                start = j * 2 * STRIP + t * STRIP
                weight[rows_at(strip * STRIP, STRIP), :] = source[start : start + STRIP, :]
    for hop in range(GROUP):
        rows = rows_at(wrap(y + hop) * PAIR, PAIR)
        outs[hop][...] = dot_nt(cot[0], weight[rows, :]).astype(BF16)


def weight_term(pos, cot, *refs):
    parts, (keep, send, term) = refs[:GROUP], refs[GROUP:]
    y, x, y_low, core = pos[0], pos[2], pos[3], pos[4]
    for hop in range(GROUP):
        shard = wrap(y - hop)
        term[...] = dot(parts[hop][...].T, cot[0]).astype(BF16)
        for i in range(4):
            start = wrap(shard - x) * 2 * STRIP + (y_low + i // 2) % 2 * STRIP
            rows = rows_at(start, STRIP)
            value = term[i * STRIP : (i + 1) * STRIP, :]

            @pl.when(core == i % 2)
            def _(rows=rows, value=value):
                keep[rows, :] = value

            @pl.when(core != i % 2)
            def _(rows=rows, value=value):
                send[rows, :] = value


def project(pos, weight, *refs):
    parts, attended = refs[:GROUP], refs[GROUP]
    y = pos[0]
    for block in range(3):
        columns = slice(block * 512, (block + 1) * 512)
        total = jnp.zeros((ROWS, 512), F32)
        for hop in range(GROUP):
            rows = rows_at(wrap(y - hop) * PAIR, PAIR)
            total = total + dot(parts[hop][...], weight[rows, columns])
        attended[0, :, columns] = total.astype(BF16)


def add_cores(keep, received, *outs):
    for j in range(4):
        rows = slice(j * 2 * STRIP, (j + 1) * 2 * STRIP)
        outs[j][...] = (keep[rows, :].astype(F32) + received[rows, :].astype(F32)).astype(BF16)


def add_x(a, b, c, d, keep, send):
    total = a[...].astype(F32) + b[...].astype(F32) + c[...].astype(F32) + d[...].astype(F32)
    keep[...] = total[0:STRIP, :]
    send[...] = total[STRIP : 2 * STRIP, :].astype(BF16)


def add_y_low(keep, received, out):
    total = (keep[...] + received[...].astype(F32)).astype(BF16)
    for j in range(out.shape[0]):
        out[j, :, :] = total[:, j * PAIR : (j + 1) * PAIR]


def add_z(parts, out):
    total = parts[0].astype(F32)
    for j in range(1, parts.shape[0]):
        total = total + parts[j].astype(F32)
    total = total.astype(BF16)
    for j in range(GROUP):
        out[j, :, :] = total[:, j * STRIP : (j + 1) * STRIP]


def add_y(parts, out):
    total = parts[0].astype(F32)
    for j in range(1, GROUP):
        total = total + parts[j].astype(F32)
    out[...] = total


def on_device(queries, keys, values, rec_lengths, out_weight, cotangent):
    n_seq = lax.axis_size("seq")
    n_z = n_seq // GROUP
    frames = n_seq * ROWS
    seq_index = lax.axis_index("seq")
    strip_index = lax.axis_index("fsdp")
    pos = jnp.stack(
        [
            seq_index % GROUP,
            seq_index // GROUP,
            strip_index // 4,
            strip_index // 2 % 2,
            strip_index % 2,
        ]
    ).astype(jnp.int32)

    def along_y(block, hop):
        route = [(i, i // GROUP * GROUP + (i + hop) % GROUP) for i in range(n_seq)]
        return lax.ppermute(block, "seq", route)

    def along_z(block, hop):
        moved = hop * GROUP
        route = [(i, i + moved) for i in range(n_seq) if 0 <= i + moved < n_seq]
        return lax.ppermute(block, "seq", route)

    def along_x(block, hop):
        return lax.ppermute(block, "fsdp", [(i, (i + 4 * hop) % 16) for i in range(16)])

    def swap_y_low(block):
        return lax.ppermute(block, "fsdp", [(i, i ^ 2) for i in range(16)])

    def swap_core(block):
        return lax.ppermute(block, "fsdp", [(i, i ^ 1) for i in range(16)])

    def exchange(chunks):
        return [chunks[0]] + [along_y(chunks[hop], hop) for hop in range(1, GROUP)]

    chunk = struct((ROWS, 3 * PAIR))
    packed = call(pack_heads, (chunk,) * GROUP, (pos, queries, keys, values))
    parts = exchange(packed)
    strips = jnp.concatenate([out_weight, swap_y_low(out_weight)], axis=0)
    mine = jnp.concatenate([strips] + [along_x(strips, hop) for hop in (1, 2, 3)], axis=0)
    other = swap_core(mine)

    edge = struct((REACH, 2 * PAIR))
    low, high = call(pack_edges, (edge, edge), (pos, *parts))
    after, before = along_z(low, -1), along_z(high, 1)

    square = struct((ROWS, PAIR))
    *grads, weight = call(
        context_grad,
        (square,) * GROUP + (struct((INNER, WIDTH)),),
        (pos, cotangent, mine, other),
        flops=2 * ROWS * INNER * WIDTH,
    )
    pair_flops = 2 * 2 * OWN * WINDOW * PAIR
    *context_parts, q_all, k_all, v_all, context, log_total = call(
        lambda *refs: forward(frames, *refs),
        (square,) * GROUP
        + (
            struct((OWN, PAIR)),
            struct((SPAN, PAIR)),
            struct((SPAN, PAIR)),
            struct((OWN, PAIR)),
            struct((OWN, 128), F32),
        ),
        (pos, rec_lengths, *parts, before, after),
        flops=2 * pair_flops,
        smem=2,
    )
    grads = exchange(grads)
    context_parts = exchange(context_parts)

    half = struct((INNER // 2, WIDTH))
    keep, send = call(
        weight_term,
        (half, half),
        (pos, cotangent, *context_parts),
        flops=2 * ROWS * INNER * WIDTH,
        scratch=[pltpu.VMEM((PAIR, WIDTH), BF16)],
    )
    received = swap_core(send)

    dq, own, low, high = call(
        lambda *refs: backward(frames, *refs),
        (struct((OWN, PAIR)), struct((OWN, 2 * PAIR), F32), edge, edge),
        (pos, rec_lengths, *grads, q_all, k_all, v_all, context, log_total),
        flops=5 * pair_flops,
        scratch=[
            pltpu.VMEM((OWN, PAIR), BF16),
            pltpu.VMEM((PAIR, SPAN), F32),
            pltpu.VMEM((PAIR, SPAN), F32),
        ],
        smem=2,
    )
    from_after, from_before = along_z(low, -1), along_z(high, 1)

    sums = call(add_cores, (struct((2 * STRIP, WIDTH)),) * 4, (keep, received), smem=0)
    sums = [sums[0]] + [along_x(sums[hop], hop) for hop in (1, 2, 3)]
    keep, send = call(
        add_x, (struct((STRIP, WIDTH), F32), struct((STRIP, WIDTH))), tuple(sums), smem=0
    )
    received = swap_y_low(send)

    attended = call(
        project,
        struct((1, ROWS, WIDTH)),
        (pos, weight, *context_parts),
        flops=2 * ROWS * INNER * WIDTH,
    )

    outs = call(
        pack_grads,
        (chunk,) * GROUP,
        (pos, dq, own, from_before, from_after),
        scratch=[pltpu.VMEM((OWN, 2 * PAIR), F32)],
    )
    outs = exchange(outs)
    full = struct((1, ROWS, INNER))
    grad_queries, grad_keys, grad_values = call(unpack_grads, (full, full, full), (pos, *outs))

    z_groups = [[z * GROUP + y for z in range(n_z)] for y in range(GROUP)]
    y_groups = [[z * GROUP + y for y in range(GROUP)] for z in range(n_z)]
    blocks = call(add_y_low, struct((n_z, STRIP, PAIR)), (keep, received), smem=0)
    blocks = lax.all_to_all(blocks, "seq", 0, 0, axis_index_groups=z_groups)
    blocks = call(add_z, struct((GROUP, STRIP, STRIP)), (blocks,), smem=0)
    blocks = lax.all_to_all(blocks, "seq", 0, 0, axis_index_groups=y_groups)
    grad_weight = call(add_y, struct((STRIP, STRIP), F32), (blocks,), smem=0)
    return attended, grad_queries, grad_keys, grad_values, grad_weight


def solution(mesh):
    rows = P("fsdp", "seq", None)
    return jax.shard_map(
        on_device,
        mesh=mesh,
        in_specs=(rows, rows, rows, P("fsdp", None), P("fsdp", None), rows),
        out_specs=(rows, rows, rows, rows, P("fsdp", "seq")),
        check_vma=False,
    )
```

```python
import jax
import jax.numpy as jnp
from jax import lax
from jax.experimental import pallas as pl
from jax.experimental.pallas import tpu as pltpu
from jax.sharding import PartitionSpec as P

HEAD_DIM = 96
ROWS = 192
GROUP = 4
PAIR = 2 * HEAD_DIM
INNER = GROUP * PAIR
OWN = GROUP * ROWS
REACH = 2 * ROWS
SPAN = OWN + 2 * REACH
TILE = 256
WINDOW = TILE + 2 * REACH
STRIP = 48
WIDTH = 1536
SCALE = HEAD_DIM ** (-0.5)
LOG2E = 1.4426950408889634
NEG_FILL = -1e30
BF16 = jnp.bfloat16
F32 = jnp.float32


def struct(shape, dtype=BF16):
    return jax.ShapeDtypeStruct(shape, dtype)


def call(body, out_shape, args, flops=0, scratch=(), smem=1, near=False):
    scalars = pl.BlockSpec(memory_space=pltpu.SMEM)

    def whole(a):
        if near:
            return pl.BlockSpec(memory_space=pltpu.VMEM)
        return pl.BlockSpec(a.shape, lambda step: (0,) * len(a.shape))

    moved = sum(a.size * a.dtype.itemsize for a in args)
    moved += sum(o.size * o.dtype.itemsize for o in jax.tree.leaves(out_shape))
    return pl.pallas_call(
        body,
        out_shape=out_shape,
        grid=() if near else (1,),
        in_specs=[scalars] * smem + [whole(a) for a in args[smem:]],
        out_specs=jax.tree.map(whole, out_shape),
        scratch_shapes=list(scratch),
        cost_estimate=pl.CostEstimate(flops=flops, bytes_accessed=moved, transcendentals=0),
        compiler_params=pltpu.CompilerParams(
            vmem_limit_bytes=(16 if near else 60) * 1024 * 1024
        ),
    )(*args)


def wrap(index):
    return lax.rem(index + 2 * GROUP, GROUP)


def rows_at(start, size):
    return pl.ds(pl.multiple_of(start, 16), size)


def dot(a, b):
    return jnp.dot(a, b, preferred_element_type=F32)


def dot_nt(a, b):
    return lax.dot_general(a, b, (((1,), (1,)), ((), ())), preferred_element_type=F32)


def pack_heads(q, k, v, out):
    for pair in range(GROUP):
        columns = slice(pair * PAIR, (pair + 1) * PAIR)
        rows = slice(pair * ROWS, (pair + 1) * ROWS)
        out[rows, 0:PAIR] = k[0, :, columns]
        out[rows, PAIR : 2 * PAIR] = v[0, :, columns]
        out[rows, 2 * PAIR : 3 * PAIR] = q[0, :, columns]


def pack_edges(parts, low, high):
    low[...] = parts[0:REACH, 0 : 2 * PAIR]
    high[...] = parts[OWN - REACH : OWN, 0 : 2 * PAIR]


def tile_mask(lengths, first_query, frames):
    query = first_query + lax.broadcasted_iota(jnp.int32, (TILE, 1), 0)
    low = jnp.maximum(query - REACH, 0)
    high = jnp.minimum(query + REACH, frames - 1)
    end = 0
    for recording in range(3):
        end = end + lengths[0, recording]
        low = jnp.maximum(low, jnp.where(query >= end, end, 0))
        high = jnp.minimum(high, jnp.where(query < end, end - 1, frames - 1))
    key = first_query - REACH + lax.broadcasted_iota(jnp.int32, (1, WINDOW), 1)
    return (key >= low) & (key <= high)


def head_columns(head):
    lane = lax.broadcasted_iota(jnp.int32, (1, PAIR), 1)
    return (lane >= head * HEAD_DIM) & (lane < (head + 1) * HEAD_DIM)


def forward(frames, pos, lengths, parts, before, after, q_all, k_all, v_all, context, log_total):
    z = pos[1]
    k_all[0:REACH, :] = before[:, 0:PAIR]
    v_all[0:REACH, :] = before[:, PAIR : 2 * PAIR]
    k_all[REACH + OWN : SPAN, :] = after[:, 0:PAIR]
    v_all[REACH + OWN : SPAN, :] = after[:, PAIR : 2 * PAIR]
    k_all[REACH : REACH + OWN, :] = parts[:, 0:PAIR]
    v_all[REACH : REACH + OWN, :] = parts[:, PAIR : 2 * PAIR]
    q_all[...] = parts[:, 2 * PAIR : 3 * PAIR]

    def step(tile, _):
        first = pl.multiple_of(tile * TILE, TILE)
        mask = tile_mask(lengths, z * OWN + first, frames)
        query = q_all[pl.ds(first, TILE), :]
        keys = k_all[pl.ds(first, WINDOW), :]
        values = v_all[pl.ds(first, WINDOW), :]
        lane = lax.broadcasted_iota(jnp.int32, (TILE, 128), 1)
        total = jnp.zeros((TILE, PAIR), F32)
        logs = jnp.zeros((TILE, 128), F32)
        for head in range(2):
            inside = head_columns(head)
            scores = dot_nt(jnp.where(inside, query, 0), keys)
            scores = jnp.where(mask, scores, NEG_FILL)
            largest = jnp.max(scores, axis=1, keepdims=True)
            expo = jnp.exp2((scores - largest) * (SCALE * LOG2E))
            sums = jnp.sum(expo, axis=1, keepdims=True)
            product = dot(expo.astype(BF16), values) / sums
            total = jnp.where(inside, product, total)
            logs = jnp.where(lane == head, largest + jnp.log(sums) * (1.0 / SCALE), logs)
        context[pl.ds(first, TILE), :] = total.astype(BF16)
        log_total[pl.ds(first, TILE), :] = logs
        return 0

    lax.fori_loop(0, OWN // TILE, step, 0)


def backward(frames, pos, lengths, q_all, k_all, v_all, context, log_total, *refs):
    parts = refs[:GROUP]
    dq, own, low, high, dk, dv, dcontext = refs[GROUP:]
    y = pos[0]
    for hop in range(GROUP):
        dcontext[rows_at(wrap(y - hop) * ROWS, ROWS), :] = parts[hop][...]
    z = pos[1]
    dk[...] = jnp.zeros_like(dk)
    dv[...] = jnp.zeros_like(dv)

    def step(tile, _):
        first = pl.multiple_of(tile * TILE, TILE)
        mask = tile_mask(lengths, z * OWN + first, frames)
        query = q_all[pl.ds(first, TILE), :]
        keys = k_all[pl.ds(first, WINDOW), :]
        values = v_all[pl.ds(first, WINDOW), :]
        grads = dcontext[pl.ds(first, TILE), :]
        product = grads.astype(F32) * context[pl.ds(first, TILE), :].astype(F32)
        logs = log_total[pl.ds(first, TILE), :]
        query_t = query.T
        grads_t = grads.T
        total = jnp.zeros((TILE, PAIR), F32)
        for head in range(2):
            inside = head_columns(head)
            own_rows = slice(head * HEAD_DIM, (head + 1) * HEAD_DIM)
            delta = jnp.sum(jnp.where(inside, product, 0.0), axis=1, keepdims=True)
            scores = dot_nt(jnp.where(inside, query, 0), keys)
            scores = jnp.where(mask, scores, NEG_FILL)
            probability = jnp.exp2((scores - logs[:, head : head + 1]) * (SCALE * LOG2E))
            gap = dot_nt(jnp.where(inside, grads, 0), values) - delta
            score_grad = (probability * gap).astype(BF16)
            total = jnp.where(inside, dot(score_grad, keys), total)
            dk[own_rows, pl.ds(first, WINDOW)] += dot(query_t[own_rows, :], score_grad)
            dv[own_rows, pl.ds(first, WINDOW)] += dot(
                grads_t[own_rows, :], probability.astype(BF16)
            )
        dq[pl.ds(first, TILE), :] = (total * SCALE).astype(BF16)
        return 0

    lax.fori_loop(0, OWN // TILE, step, 0)
    low[:, 0:PAIR] = (dk[:, 0:REACH].T * SCALE).astype(BF16)
    low[:, PAIR : 2 * PAIR] = dv[:, 0:REACH].T.astype(BF16)
    high[:, 0:PAIR] = (dk[:, REACH + OWN : SPAN].T * SCALE).astype(BF16)
    high[:, PAIR : 2 * PAIR] = dv[:, REACH + OWN : SPAN].T.astype(BF16)
    own[:, 0:PAIR] = dk[:, REACH : REACH + OWN].T * SCALE
    own[:, PAIR : 2 * PAIR] = dv[:, REACH : REACH + OWN].T


def pack_grads(pos, dq, own, from_before, from_after, *refs):
    outs, total = refs[:GROUP], refs[GROUP]
    y = pos[0]
    first, last = slice(0, REACH), slice(REACH, OWN)
    total[first, :] = own[first, :] + from_before[...].astype(F32)
    total[last, :] = own[last, :] + from_after[...].astype(F32)
    for hop in range(GROUP):
        rows = rows_at(wrap(y + hop) * ROWS, ROWS)
        outs[hop][:, 0 : 2 * PAIR] = total[rows, :].astype(BF16)
        outs[hop][:, 2 * PAIR : 3 * PAIR] = dq[rows, :]


def unpack_grads(pos, *refs):
    parts, (dq, dk, dv) = refs[:GROUP], refs[GROUP:]
    y = pos[0]
    for hop in range(GROUP):
        shard = wrap(y - hop)
        for pair in range(GROUP):

            @pl.when(shard == pair)
            def _(hop=hop, pair=pair):
                columns = slice(pair * PAIR, (pair + 1) * PAIR)
                dk[0, :, columns] = parts[hop][:, 0:PAIR]
                dv[0, :, columns] = parts[hop][:, PAIR : 2 * PAIR]
                dq[0, :, columns] = parts[hop][:, 2 * PAIR : 3 * PAIR]


def join(*refs):
    parts, out = refs[:-1], refs[-1]
    size = parts[0].shape[0]
    for j, part in enumerate(parts):
        out[j * size : (j + 1) * size, :] = part[...]


def context_grad(pos, cot, mine, other, weight, *outs):
    y, x, y_low, core = pos[0], pos[2], pos[3], pos[4]
    for j in range(4):
        for t in range(2):
            for flip, source in ((0, mine), (1, other)):
                strip = wrap(x - j) * 4 + (y_low + t) % 2 * 2 + (core + flip) % 2
                start = j * 2 * STRIP + t * STRIP
                weight[rows_at(strip * STRIP, STRIP), :] = source[start : start + STRIP, :]
    for hop in range(GROUP):
        rows = rows_at(wrap(y + hop) * PAIR, PAIR)
        outs[hop][...] = dot_nt(cot[0], weight[rows, :]).astype(BF16)


def weight_term(pos, cot, context, keep, send):
    core = pos[4]
    for pair in range(GROUP):
        part = context[pair * ROWS : (pair + 1) * ROWS, :]
        term = dot(part.T, cot[0]).astype(BF16)
        for i in range(4):
            start = (pair * 2 + i // 2) * STRIP
            rows = slice(start, start + STRIP)
            value = term[i * STRIP : (i + 1) * STRIP, :]

            @pl.when(core == i % 2)
            def _(rows=rows, value=value):
                keep[rows, :] = value

            @pl.when(core != i % 2)
            def _(rows=rows, value=value):
                send[rows, :] = value


def project(weight, context, attended):
    for block in range(3):
        columns = slice(block * 512, (block + 1) * 512)
        total = jnp.zeros((ROWS, 512), F32)
        for pair in range(GROUP):
            rows = slice(pair * ROWS, (pair + 1) * ROWS)
            total = total + dot(context[rows, :], weight[rows, columns])
        attended[0, :, columns] = total.astype(BF16)


def add_cores(keep, received, out):
    out[...] = (keep[...].astype(F32) + received[...].astype(F32)).astype(BF16)


def added(parts, size):
    total = parts[0:size, :].astype(F32)
    for j in range(1, parts.shape[0] // size):
        total = total + parts[j * size : (j + 1) * size, :].astype(F32)
    return total


def add_x(parts, out):
    total = added(parts, 2 * STRIP).astype(BF16)
    for shard in range(GROUP):
        for strip in range(2):
            start = (shard * 2 + strip) * STRIP
            value = total[strip * STRIP : (strip + 1) * STRIP, :]
            for z in range(out.shape[1] // STRIP):
                source = (z * GROUP + shard) * STRIP
                out[start : start + STRIP, z * STRIP : (z + 1) * STRIP] = value[
                    :, source : source + STRIP
                ]


def add_y(parts, out):
    total = added(parts, STRIP).astype(BF16)
    out[...] = jnp.zeros_like(out)
    for z in range(total.shape[1] // STRIP):
        out[z * STRIP : (z + 1) * STRIP, 0:STRIP] = total[:, z * STRIP : (z + 1) * STRIP]


def add_z(parts, out):
    out[...] = added(parts, STRIP)[:, 0:STRIP]


def on_device(queries, keys, values, rec_lengths, out_weight, cotangent):
    n_seq = lax.axis_size("seq")
    n_z = n_seq // GROUP
    frames = n_seq * ROWS
    seq_index = lax.axis_index("seq")
    strip_index = lax.axis_index("fsdp")
    pos = jnp.stack(
        [
            seq_index % GROUP,
            seq_index // GROUP,
            strip_index // 4,
            strip_index // 2 % 2,
            strip_index % 2,
        ]
    ).astype(jnp.int32)
    y_groups = [[z * GROUP + y for y in range(GROUP)] for z in range(n_z)]
    x_groups = [[x * 4 + rest for x in range(4)] for rest in range(4)]
    z_groups = [[z * GROUP + y for z in range(n_z)] for y in range(GROUP)]
    whole_y_groups = [
        [(z * GROUP + y) * 16 + x * 4 + y_low * 2 + core for y in range(GROUP) for y_low in range(2)]
        for z in range(n_z)
        for x in range(4)
        for core in range(2)
    ]

    def exchange(block, axis="seq", groups=y_groups):
        return lax.all_to_all(block, axis, 0, 0, axis_index_groups=groups, tiled=True)

    def along_z(block, hop):
        moved = hop * GROUP
        route = [(i, i + moved) for i in range(n_seq) if 0 <= i + moved < n_seq]
        return lax.ppermute(block, "seq", route)

    def along_y(block, hop):
        route = [(i, i // GROUP * GROUP + (i + hop) % GROUP) for i in range(n_seq)]
        return lax.ppermute(block, "seq", route)

    def along_x(block, hop):
        return lax.ppermute(block, "fsdp", [(i, (i + 4 * hop) % 16) for i in range(16)])

    def swap_y_low(block):
        return lax.ppermute(block, "fsdp", [(i, i ^ 2) for i in range(16)])

    def swap_core(block):
        return lax.ppermute(block, "fsdp", [(i, i ^ 1) for i in range(16)])

    def spread(chunks):
        return [chunks[0]] + [along_y(chunks[hop], hop) for hop in range(1, GROUP)]

    together = lax.optimization_barrier
    half = struct((INNER // 2, WIDTH))
    edge = struct((REACH, 2 * PAIR))
    square = struct((OWN, PAIR))
    span = struct((SPAN, PAIR))
    chunk = struct((ROWS, 3 * PAIR))
    full = struct((1, ROWS, INNER))
    pair_flops = 2 * 2 * OWN * WINDOW * PAIR
    project_flops = 2 * ROWS * INNER * WIDTH

    packed = call(pack_heads, struct((OWN, 3 * PAIR)), (queries, keys, values), smem=0)
    other_strip = swap_y_low(out_weight)
    packed, other_strip = together((packed, other_strip))
    parts = exchange(packed)
    strips = call(
        join, struct((2 * STRIP, WIDTH)), (out_weight, other_strip), smem=0, near=True
    )
    weights = [along_x(strips, hop) for hop in (1, 2, 3)]
    parts, weights = together((parts, weights))

    low, high = call(pack_edges, (edge, edge), (parts,), smem=0, near=True)
    after, before = along_z(low, -1), along_z(high, 1)
    mine = call(join, half, (strips, *weights), smem=0, near=True)
    mine, before, after = together((mine, before, after))
    other = swap_core(mine)
    q_all, k_all, v_all, context, log_total = call(
        lambda *refs: forward(frames, *refs),
        (square, span, span, square, struct((OWN, 128), F32)),
        (pos, rec_lengths, parts, before, after),
        flops=2 * pair_flops,
        smem=2,
    )
    context_rows = exchange(context)
    mine, context = together((mine, context))
    weight, *grads = call(
        context_grad,
        (struct((INNER, WIDTH)),) + (struct((ROWS, PAIR)),) * GROUP,
        (pos, cotangent, mine, other),
        flops=project_flops,
    )
    grads = spread(grads)
    context_rows, grads = together((context_rows, grads))

    keep, send = call(
        weight_term, (half, half), (pos, cotangent, context_rows), flops=project_flops
    )
    received = swap_core(send)
    keep, grads, context_rows = together((keep, grads, context_rows))
    dq, own, low, high = call(
        lambda *refs: backward(frames, *refs),
        (square, struct((OWN, 2 * PAIR), F32), edge, edge),
        (pos, rec_lengths, q_all, k_all, v_all, context, log_total, *grads),
        flops=5 * pair_flops,
        scratch=[
            pltpu.VMEM((PAIR, SPAN), F32),
            pltpu.VMEM((PAIR, SPAN), F32),
            pltpu.VMEM((OWN, PAIR), BF16),
        ],
        smem=2,
    )
    received, low, high = together((received, low, high))
    from_after, from_before = along_z(low, -1), along_z(high, 1)
    sums = call(add_cores, half, (keep, received), smem=0)
    sums = exchange(sums, "fsdp", x_groups)
    chunks = call(
        pack_grads,
        (chunk,) * GROUP,
        (pos, dq, own, from_before, from_after),
        scratch=[pltpu.VMEM((OWN, 2 * PAIR), F32)],
    )
    sums, chunks = together((sums, chunks))
    sums = call(add_x, struct((2 * GROUP * STRIP, n_z * STRIP)), (sums,), smem=0, near=True)
    grads = spread(chunks)
    sums = exchange(sums, ("seq", "fsdp"), whole_y_groups)
    sums = call(add_y, struct((n_z * STRIP, 128)), (sums,), smem=0, near=True)
    sums, context_rows = together((sums, context_rows))
    sums = exchange(sums, "seq", z_groups)
    attended = call(
        project, struct((1, ROWS, WIDTH)), (weight, context_rows), flops=project_flops, smem=0
    )
    attended, grads = together((attended, grads))
    grad_queries, grad_keys, grad_values = call(unpack_grads, (full, full, full), (pos, *grads))
    sums, grad_queries = together((sums, grad_queries))
    grad_weight = call(add_z, struct((STRIP, STRIP), F32), (sums,), smem=0, near=True)
    return attended, grad_queries, grad_keys, grad_values, grad_weight


def solution(mesh):
    rows = P("fsdp", "seq", None)
    return jax.shard_map(
        on_device,
        mesh=mesh,
        in_specs=(rows, rows, rows, P("fsdp", None), P("fsdp", None), rows),
        out_specs=(rows, rows, rows, rows, P("fsdp", "seq")),
        check_vma=False,
    )
```

```python
import jax
import jax.numpy as jnp
from jax import lax
from jax.experimental import pallas as pl
from jax.experimental.pallas import tpu as pltpu
from jax.sharding import PartitionSpec as P

HEAD_DIM = 96
ROWS = 192
GROUP = 4
PAIR = 2 * HEAD_DIM
INNER = GROUP * PAIR
OWN = GROUP * ROWS
REACH = 2 * ROWS
SPAN = OWN + 2 * REACH
TILE = 256
WINDOW = TILE + 2 * REACH
STRIP = 48
WIDTH = 1536
SCALE = HEAD_DIM ** (-0.5)
LOG2E = 1.4426950408889634
NEG_FILL = -1e30
BF16 = jnp.bfloat16
F32 = jnp.float32


def struct(shape, dtype=BF16):
    return jax.ShapeDtypeStruct(shape, dtype)


def call(body, out_shape, args, flops=0, scratch=(), smem=1, near=False):
    scalars = pl.BlockSpec(memory_space=pltpu.SMEM)

    def whole(a):
        if near:
            return pl.BlockSpec(memory_space=pltpu.VMEM)
        return pl.BlockSpec(a.shape, lambda step: (0,) * len(a.shape))

    moved = sum(a.size * a.dtype.itemsize for a in args)
    moved += sum(o.size * o.dtype.itemsize for o in jax.tree.leaves(out_shape))
    return pl.pallas_call(
        body,
        out_shape=out_shape,
        grid=() if near else (1,),
        in_specs=[scalars] * smem + [whole(a) for a in args[smem:]],
        out_specs=jax.tree.map(whole, out_shape),
        scratch_shapes=list(scratch),
        cost_estimate=pl.CostEstimate(flops=flops, bytes_accessed=moved, transcendentals=0),
        compiler_params=pltpu.CompilerParams(
            vmem_limit_bytes=(16 if near else 60) * 1024 * 1024
        ),
    )(*args)


def wrap(index):
    return lax.rem(index + 2 * GROUP, GROUP)


def rows_at(start, size):
    return pl.ds(pl.multiple_of(start, 16), size)


def dot(a, b):
    return jnp.dot(a, b, preferred_element_type=F32)


def dot_nt(a, b):
    return lax.dot_general(a, b, (((1,), (1,)), ((), ())), preferred_element_type=F32)


def pack_heads(q, k, v, out):
    for pair in range(GROUP):
        columns = slice(pair * PAIR, (pair + 1) * PAIR)
        rows = slice(pair * ROWS, (pair + 1) * ROWS)
        out[rows, 0:PAIR] = k[0, :, columns]
        out[rows, PAIR : 2 * PAIR] = v[0, :, columns]
        out[rows, 2 * PAIR : 3 * PAIR] = q[0, :, columns]


def pack_edges(parts, low, high):
    low[...] = parts[0:REACH, 0 : 2 * PAIR]
    high[...] = parts[OWN - REACH : OWN, 0 : 2 * PAIR]


def tile_mask(lengths, first_query, frames):
    query = first_query + lax.broadcasted_iota(jnp.int32, (TILE, 1), 0)
    low = jnp.maximum(query - REACH, 0)
    high = jnp.minimum(query + REACH, frames - 1)
    end = 0
    for recording in range(3):
        end = end + lengths[0, recording]
        low = jnp.maximum(low, jnp.where(query >= end, end, 0))
        high = jnp.minimum(high, jnp.where(query < end, end - 1, frames - 1))
    key = first_query - REACH + lax.broadcasted_iota(jnp.int32, (1, WINDOW), 1)
    return (key >= low) & (key <= high)


def head_columns(head):
    lane = lax.broadcasted_iota(jnp.int32, (1, PAIR), 1)
    return (lane >= head * HEAD_DIM) & (lane < (head + 1) * HEAD_DIM)


def forward(frames, pos, lengths, parts, before, after, q_all, k_all, v_all, context, log_total):
    z = pos[1]
    k_all[0:REACH, :] = before[:, 0:PAIR]
    v_all[0:REACH, :] = before[:, PAIR : 2 * PAIR]
    k_all[REACH + OWN : SPAN, :] = after[:, 0:PAIR]
    v_all[REACH + OWN : SPAN, :] = after[:, PAIR : 2 * PAIR]
    k_all[REACH : REACH + OWN, :] = parts[:, 0:PAIR]
    v_all[REACH : REACH + OWN, :] = parts[:, PAIR : 2 * PAIR]
    q_all[...] = parts[:, 2 * PAIR : 3 * PAIR]

    def step(tile, _):
        first = pl.multiple_of(tile * TILE, TILE)
        mask = tile_mask(lengths, z * OWN + first, frames)
        query = q_all[pl.ds(first, TILE), :]
        keys = k_all[pl.ds(first, WINDOW), :]
        values = v_all[pl.ds(first, WINDOW), :]
        lane = lax.broadcasted_iota(jnp.int32, (TILE, 128), 1)
        total = jnp.zeros((TILE, PAIR), F32)
        logs = jnp.zeros((TILE, 128), F32)
        for head in range(2):
            inside = head_columns(head)
            scores = dot_nt(jnp.where(inside, query, 0), keys)
            scores = jnp.where(mask, scores, NEG_FILL)
            largest = jnp.max(scores, axis=1, keepdims=True)
            expo = jnp.exp2((scores - largest) * (SCALE * LOG2E))
            sums = jnp.sum(expo, axis=1, keepdims=True)
            product = dot(expo.astype(BF16), values) / sums
            total = jnp.where(inside, product, total)
            logs = jnp.where(lane == head, largest + jnp.log(sums) * (1.0 / SCALE), logs)
        context[pl.ds(first, TILE), :] = total.astype(BF16)
        log_total[pl.ds(first, TILE), :] = logs
        return 0

    lax.fori_loop(0, OWN // TILE, step, 0)


def backward(frames, pos, lengths, q_all, k_all, v_all, context, log_total, *refs):
    parts = refs[:GROUP]
    dq, own, low, high, dk, dv, dcontext = refs[GROUP:]
    y = pos[0]
    for hop in range(GROUP):
        dcontext[rows_at(wrap(y - hop) * ROWS, ROWS), :] = parts[hop][...]
    z = pos[1]
    dk[...] = jnp.zeros_like(dk)
    dv[...] = jnp.zeros_like(dv)

    def step(tile, _):
        first = pl.multiple_of(tile * TILE, TILE)
        mask = tile_mask(lengths, z * OWN + first, frames)
        query = q_all[pl.ds(first, TILE), :]
        keys = k_all[pl.ds(first, WINDOW), :]
        values = v_all[pl.ds(first, WINDOW), :]
        grads = dcontext[pl.ds(first, TILE), :]
        product = grads.astype(F32) * context[pl.ds(first, TILE), :].astype(F32)
        logs = log_total[pl.ds(first, TILE), :]
        query_t = query.T
        grads_t = grads.T
        total = jnp.zeros((TILE, PAIR), F32)
        for head in range(2):
            inside = head_columns(head)
            own_rows = slice(head * HEAD_DIM, (head + 1) * HEAD_DIM)
            delta = jnp.sum(jnp.where(inside, product, 0.0), axis=1, keepdims=True)
            scores = dot_nt(jnp.where(inside, query, 0), keys)
            scores = jnp.where(mask, scores, NEG_FILL)
            probability = jnp.exp2((scores - logs[:, head : head + 1]) * (SCALE * LOG2E))
            gap = dot_nt(jnp.where(inside, grads, 0), values) - delta
            score_grad = (probability * gap).astype(BF16)
            total = jnp.where(inside, dot(score_grad, keys), total)
            dk[own_rows, pl.ds(first, WINDOW)] += dot(query_t[own_rows, :], score_grad)
            dv[own_rows, pl.ds(first, WINDOW)] += dot(
                grads_t[own_rows, :], probability.astype(BF16)
            )
        dq[pl.ds(first, TILE), :] = (total * SCALE).astype(BF16)
        return 0

    lax.fori_loop(0, OWN // TILE, step, 0)
    low[:, 0:PAIR] = (dk[:, 0:REACH].T * SCALE).astype(BF16)
    low[:, PAIR : 2 * PAIR] = dv[:, 0:REACH].T.astype(BF16)
    high[:, 0:PAIR] = (dk[:, REACH + OWN : SPAN].T * SCALE).astype(BF16)
    high[:, PAIR : 2 * PAIR] = dv[:, REACH + OWN : SPAN].T.astype(BF16)
    own[:, 0:PAIR] = dk[:, REACH : REACH + OWN].T * SCALE
    own[:, PAIR : 2 * PAIR] = dv[:, REACH : REACH + OWN].T


def pack_grads(pos, dq, own, from_before, from_after, *refs):
    outs, total = refs[:GROUP], refs[GROUP]
    y = pos[0]
    first, last = slice(0, REACH), slice(REACH, OWN)
    total[first, :] = own[first, :] + from_before[...].astype(F32)
    total[last, :] = own[last, :] + from_after[...].astype(F32)
    for hop in range(GROUP):
        rows = rows_at(wrap(y + hop) * ROWS, ROWS)
        outs[hop][:, 0 : 2 * PAIR] = total[rows, :].astype(BF16)
        outs[hop][:, 2 * PAIR : 3 * PAIR] = dq[rows, :]


def unpack_grads(pos, *refs):
    parts, (dq, dk, dv) = refs[:GROUP], refs[GROUP:]
    y = pos[0]
    for hop in range(GROUP):
        shard = wrap(y - hop)
        for pair in range(GROUP):

            @pl.when(shard == pair)
            def _(hop=hop, pair=pair):
                columns = slice(pair * PAIR, (pair + 1) * PAIR)
                dk[0, :, columns] = parts[hop][:, 0:PAIR]
                dv[0, :, columns] = parts[hop][:, PAIR : 2 * PAIR]
                dq[0, :, columns] = parts[hop][:, 2 * PAIR : 3 * PAIR]


def join(*refs):
    parts, out = refs[:-1], refs[-1]
    size = parts[0].shape[0]
    for j, part in enumerate(parts):
        out[j * size : (j + 1) * size, :] = part[...]


def context_grad(pos, cot, mine, other, weight, *outs):
    y, x, y_low, core = pos[0], pos[2], pos[3], pos[4]
    for j in range(4):
        for t in range(2):
            for flip, source in ((0, mine), (1, other)):
                strip = wrap(x - j) * 4 + (y_low + t) % 2 * 2 + (core + flip) % 2
                start = j * 2 * STRIP + t * STRIP
                weight[rows_at(strip * STRIP, STRIP), :] = source[start : start + STRIP, :]
    for hop in range(GROUP):
        rows = rows_at(wrap(y + hop) * PAIR, PAIR)
        outs[hop][...] = dot_nt(cot[0], weight[rows, :]).astype(BF16)


def weight_term(pos, cot, context, keep, send):
    core = pos[4]
    for pair in range(GROUP):
        part = context[pair * ROWS : (pair + 1) * ROWS, :]
        term = dot(part.T, cot[0]).astype(BF16)
        for i in range(4):
            start = (pair * 2 + i // 2) * STRIP
            rows = slice(start, start + STRIP)
            value = term[i * STRIP : (i + 1) * STRIP, :]

            @pl.when(core == i % 2)
            def _(rows=rows, value=value):
                keep[rows, :] = value

            @pl.when(core != i % 2)
            def _(rows=rows, value=value):
                send[rows, :] = value


def project(weight, context, attended):
    for block in range(3):
        columns = slice(block * 512, (block + 1) * 512)
        total = jnp.zeros((ROWS, 512), F32)
        for pair in range(GROUP):
            rows = slice(pair * ROWS, (pair + 1) * ROWS)
            total = total + dot(context[rows, :], weight[rows, columns])
        attended[0, :, columns] = total.astype(BF16)


def add_cores(keep, received, out):
    out[...] = (keep[...].astype(F32) + received[...].astype(F32)).astype(BF16)


def added(parts, size):
    total = parts[0:size, :].astype(F32)
    for j in range(1, parts.shape[0] // size):
        total = total + parts[j * size : (j + 1) * size, :].astype(F32)
    return total


def add_x(parts, out):
    total = added(parts, 2 * STRIP).astype(BF16)
    for shard in range(GROUP):
        for strip in range(2):
            start = (shard * 2 + strip) * STRIP
            value = total[strip * STRIP : (strip + 1) * STRIP, :]
            for z in range(out.shape[1] // STRIP):
                source = (z * GROUP + shard) * STRIP
                out[start : start + STRIP, z * STRIP : (z + 1) * STRIP] = value[
                    :, source : source + STRIP
                ]


def add_y(parts, out):
    total = added(parts, STRIP).astype(BF16)
    out[...] = jnp.zeros_like(out)
    for z in range(total.shape[1] // STRIP):
        out[z * STRIP : (z + 1) * STRIP, 0:STRIP] = total[:, z * STRIP : (z + 1) * STRIP]


def add_z(parts, out):
    out[...] = added(parts, STRIP)[:, 0:STRIP]


def on_device(queries, keys, values, rec_lengths, out_weight, cotangent):
    n_seq = lax.axis_size("seq")
    n_z = n_seq // GROUP
    frames = n_seq * ROWS
    seq_index = lax.axis_index("seq")
    strip_index = lax.axis_index("fsdp")
    pos = jnp.stack(
        [
            seq_index % GROUP,
            seq_index // GROUP,
            strip_index // 4,
            strip_index // 2 % 2,
            strip_index % 2,
        ]
    ).astype(jnp.int32)
    y_groups = [[z * GROUP + y for y in range(GROUP)] for z in range(n_z)]
    x_groups = [[x * 4 + rest for x in range(4)] for rest in range(4)]
    z_groups = [[z * GROUP + y for z in range(n_z)] for y in range(GROUP)]
    whole_y_groups = [
        [(z * GROUP + y) * 16 + x * 4 + y_low * 2 + core for y in range(GROUP) for y_low in range(2)]
        for z in range(n_z)
        for x in range(4)
        for core in range(2)
    ]

    def exchange(block, axis="seq", groups=y_groups):
        return lax.all_to_all(block, axis, 0, 0, axis_index_groups=groups, tiled=True)

    def along_z(block, hop):
        moved = hop * GROUP
        route = [(i, i + moved) for i in range(n_seq) if 0 <= i + moved < n_seq]
        return lax.ppermute(block, "seq", route)

    def along_y(block, hop):
        route = [(i, i // GROUP * GROUP + (i + hop) % GROUP) for i in range(n_seq)]
        return lax.ppermute(block, "seq", route)

    def along_x(block, hop):
        return lax.ppermute(block, "fsdp", [(i, (i + 4 * hop) % 16) for i in range(16)])

    def swap_y_low(block):
        return lax.ppermute(block, "fsdp", [(i, i ^ 2) for i in range(16)])

    def swap_core(block):
        return lax.ppermute(block, "fsdp", [(i, i ^ 1) for i in range(16)])

    def spread(chunks):
        return [chunks[0]] + [along_y(chunks[hop], hop) for hop in range(1, GROUP)]

    together = lax.optimization_barrier
    half = struct((INNER // 2, WIDTH))
    edge = struct((REACH, 2 * PAIR))
    square = struct((OWN, PAIR))
    span = struct((SPAN, PAIR))
    chunk = struct((ROWS, 3 * PAIR))
    full = struct((1, ROWS, INNER))
    pair_flops = 2 * 2 * OWN * WINDOW * PAIR
    project_flops = 2 * ROWS * INNER * WIDTH

    packed = call(pack_heads, struct((OWN, 3 * PAIR)), (queries, keys, values), smem=0)
    other_strip = swap_y_low(out_weight)
    packed, other_strip = together((packed, other_strip))
    parts = exchange(packed)
    strips = call(
        join, struct((2 * STRIP, WIDTH)), (out_weight, other_strip), smem=0, near=True
    )
    weights = [along_x(strips, hop) for hop in (1, 2, 3)]
    parts, weights = together((parts, weights))

    low, high = call(pack_edges, (edge, edge), (parts,), smem=0, near=True)
    after, before = along_z(low, -1), along_z(high, 1)
    mine = call(join, half, (strips, *weights), smem=0, near=True)
    mine, before, after = together((mine, before, after))
    other = swap_core(mine)
    q_all, k_all, v_all, context, log_total = call(
        lambda *refs: forward(frames, *refs),
        (square, span, span, square, struct((OWN, 128), F32)),
        (pos, rec_lengths, parts, before, after),
        flops=2 * pair_flops,
        smem=2,
    )
    context_rows = exchange(context)
    mine, context = together((mine, context))
    weight, *grads = call(
        context_grad,
        (struct((INNER, WIDTH)),) + (struct((ROWS, PAIR)),) * GROUP,
        (pos, cotangent, mine, other),
        flops=project_flops,
    )
    grads = spread(grads)
    context_rows, grads = together((context_rows, grads))

    keep, send = call(
        weight_term, (half, half), (pos, cotangent, context_rows), flops=project_flops
    )
    received = swap_core(send)
    keep, grads, context_rows = together((keep, grads, context_rows))
    dq, own, low, high = call(
        lambda *refs: backward(frames, *refs),
        (square, struct((OWN, 2 * PAIR), F32), edge, edge),
        (pos, rec_lengths, q_all, k_all, v_all, context, log_total, *grads),
        flops=5 * pair_flops,
        scratch=[
            pltpu.VMEM((PAIR, SPAN), F32),
            pltpu.VMEM((PAIR, SPAN), F32),
            pltpu.VMEM((OWN, PAIR), BF16),
        ],
        smem=2,
    )
    received, low, high = together((received, low, high))
    from_after, from_before = along_z(low, -1), along_z(high, 1)
    sums = call(add_cores, half, (keep, received), smem=0)
    sums, context_rows = together((sums, context_rows))
    sums = exchange(sums, "fsdp", x_groups)
    attended = call(
        project, struct((1, ROWS, WIDTH)), (weight, context_rows), flops=project_flops, smem=0
    )
    attended, from_after = together((attended, from_after))
    chunks = call(
        pack_grads,
        (chunk,) * GROUP,
        (pos, dq, own, from_before, from_after),
        scratch=[pltpu.VMEM((OWN, 2 * PAIR), F32)],
    )
    sums, chunks = together((sums, chunks))
    sums = call(add_x, struct((2 * GROUP * STRIP, n_z * STRIP)), (sums,), smem=0, near=True)
    grads = spread(chunks)
    sums = exchange(sums, ("seq", "fsdp"), whole_y_groups)
    sums = call(add_y, struct((n_z * STRIP, 128)), (sums,), smem=0, near=True)
    sums = exchange(sums, "seq", z_groups)
    grad_queries, grad_keys, grad_values = call(unpack_grads, (full, full, full), (pos, *grads))
    sums, grad_queries = together((sums, grad_queries))
    grad_weight = call(add_z, struct((STRIP, STRIP), F32), (sums,), smem=0, near=True)
    return attended, grad_queries, grad_keys, grad_values, grad_weight


def solution(mesh):
    rows = P("fsdp", "seq", None)
    return jax.shard_map(
        on_device,
        mesh=mesh,
        in_specs=(rows, rows, rows, P("fsdp", None), P("fsdp", None), rows),
        out_specs=(rows, rows, rows, rows, P("fsdp", "seq")),
        check_vma=False,
    )
```
